256 devices in a mesh: front: 16 (over y_lo, x, core), tile: 16 (over y_hi, z).
Axes of the slice: x: 4, y: 4 (y_hi: 2, y_lo: 2; y = y_hi * 2 + y_lo), z: 8, core: 2. Of those that a mesh axis runs over, the one named last changes fastest.
Arguments:
- pivot_inverse: float32 [16, 2, 512, 512], P('front', None, 'tile'), may hold values from -0.26516504 to 0.26516504
- panel_upper: float32 [16, 2, 512, 2048], P('front', None, None, 'tile'), may hold values from -6 to 6
- panel_lower: float32 [16, 2, 2048, 512], P('front', None, 'tile'), may hold values from -4.2426407 to 4.2426407
- index_map: int32 [16, 2, 2048], replicated, may hold values from 0 to 4095, as said below
- parent_base: float32 [16, 4096, 4096], P('front', None, 'tile'), may hold values from -512 to 512
Outputs:
- parent_front: float32 [16, 4096, 4096], P('front', None, 'tile')
The draws below stay inside these ranges and needn't reach their ends.
Inputs may be any that keep to these rules, and one draw needn't show every extreme that they name: Each list index_map[g, c] holds 2048 distinct parent indices in no particular order, among them 0 and 4095.
All inputs are finite; a program needn't handle non-finite values.
Results may differ from the reference program's by a relative error of at most 0.0003.
Values sent between devices are 32-bit elements; how exact they have to be, the bound alone decides.
No kernel may reach another device: no remote copies, remote signals or barrier semaphores. Data moves between devices by JAX's collectives and lax.ppermute only.
A program may use at most 128 MiB of HBM per device.

```python
import jax
import jax.numpy as jnp
from jax import lax

NP = 512
NC = 2048
NPF = 4096
CHILDREN = 2
GROUPS = 16


lower_gain = 16.0


def float_values(key, label, shape, scale):
    sub = jax.random.fold_in(key, label)
    values = jnp.clip(jax.random.normal(sub, shape, jnp.float32), -6.0, 6.0)
    return values * scale


def draw_pivot_inverse(key, part):
    return float_values(key, 11, (GROUPS, CHILDREN, NP, NP), NP ** (-0.5))


def draw_panel_upper(key, part):
    return float_values(key, 12, (GROUPS, CHILDREN, NP, NC), 1.0)


def draw_panel_lower(key, part):
    return float_values(key, 13, (GROUPS, CHILDREN, NC, NP), lower_gain * NP ** (-0.5))


def draw_index_map(key, part):
    keys = jax.random.split(jax.random.fold_in(key, 14), GROUPS * CHILDREN)

    def one_list(single):
        first_key, second_key = jax.random.split(single)
        shuffled = jax.random.permutation(first_key, NPF - 2) + 1
        chosen = shuffled[:NC - 2].astype(jnp.int32)
        first = jnp.zeros((1,), jnp.int32)
        last = jnp.full((1,), NPF - 1, jnp.int32)
        joined = jnp.concatenate([first, chosen, last])
        order = jax.random.permutation(second_key, NC)
        return joined[order].astype(jnp.int32)
    lists = jax.vmap(one_list)(keys)
    return lists.reshape(GROUPS, CHILDREN, NC).astype(jnp.int32)


def exact_block(inverse, upper, lower, mapping):
    factor = jnp.dot(inverse, upper, precision=lax.Precision.HIGHEST)
    update = jnp.dot(lower, factor, precision=lax.Precision.HIGHEST)
    extended = jnp.zeros((NPF, NPF), jnp.float32)
    return extended.at[mapping[:, None], mapping[None, :]].set(update)


def draw_parent_base(key, part):
    inverse = draw_pivot_inverse(key, part)
    upper = draw_panel_upper(key, part)
    lower = draw_panel_lower(key, part)
    mapping = draw_index_map(key, part)
    noise_key = jax.random.fold_in(key, 15)

    def one_parent(group):
        partner = jnp.bitwise_xor(group, 1).astype(jnp.int32)
        first = exact_block(inverse[group, 0], upper[group, 0], lower[group, 0], mapping[group, 0])
        second = exact_block(inverse[partner, 1], upper[partner, 1], lower[partner, 1], mapping[partner, 1])
        noise = float_values(jax.random.fold_in(noise_key, group), 16, (NPF, NPF), 1.0)
        return jnp.clip(noise + first + second, -512.0, 512.0)
    groups = jnp.arange(GROUPS, dtype=jnp.int32)
    return lax.map(one_parent, groups)


def setup_inputs(seed: int = 0) -> dict:
    key_of = jax.random.split(jax.random.key(seed), 6)
    pivot_inverse = draw_pivot_inverse(jax.random.fold_in(key_of[5], 71), 0)
    panel_upper = draw_panel_upper(jax.random.fold_in(key_of[5], 71), 0)
    panel_lower = draw_panel_lower(jax.random.fold_in(key_of[5], 71), 0)
    index_map = draw_index_map(jax.random.fold_in(key_of[5], 71), 0)
    parent_base = draw_parent_base(jax.random.fold_in(key_of[5], 71), 0)
    return {"pivot_inverse": pivot_inverse, "panel_upper": panel_upper, "panel_lower": panel_lower, "index_map": index_map, "parent_base": parent_base}


def split_parts(matrix):
    high = matrix.astype(jnp.bfloat16)
    back = lax.optimization_barrier(high).astype(jnp.float32)
    low = (matrix - back).astype(jnp.bfloat16)
    return high, low


def split_product(left, right):
    left_high, left_low = split_parts(left)
    right_high, right_low = split_parts(right)
    total = jnp.dot(left_high, right_high, preferred_element_type=jnp.float32)
    total = total + jnp.dot(left_high, right_low, preferred_element_type=jnp.float32)
    return total + jnp.dot(left_low, right_high, preferred_element_type=jnp.float32)


def child_block(pivot_inverse, panel_upper, panel_lower, index_map, group, child):
    inverse = pivot_inverse[group, child]
    upper = panel_upper[group, child]
    lower = panel_lower[group, child]
    mapping = index_map[group, child].astype(jnp.int32)
    factor = split_product(inverse, upper)
    update = split_product(lower, factor)
    return place_update(mapping, update)


def place_update(mapping, update):
    extended = jnp.zeros((NPF, NPF), jnp.float32)
    return extended.at[mapping[:, None], mapping[None, :]].set(update)


def reference(pivot_inverse, panel_upper, panel_lower, index_map, parent_base):
    def one_parent(group):
        partner = jnp.bitwise_xor(group, 1).astype(jnp.int32)
        first = child_block(pivot_inverse, panel_upper, panel_lower, index_map, group, 0)
        second = child_block(pivot_inverse, panel_upper, panel_lower, index_map, partner, 1)
        return parent_base[group] - first - second

    groups = jnp.arange(parent_base.shape[0], dtype=jnp.int32)
    return lax.map(one_parent, groups)
```

```python
import functools

import jax
import jax.numpy as jnp
from jax import lax
from jax.experimental import pallas as pl
from jax.experimental.pallas import tpu as pltpu
from jax.sharding import PartitionSpec as P

RING = 8
SLOT = 64
MIB = 1024 * 1024
F32, BF16, I32 = jnp.float32, jnp.bfloat16, jnp.int32
TRANSPOSED = (((1,), (1,)), ((), ()))


def shift(distance):
    def to(i):
        return (i // RING) * RING + (i + distance) % RING

    return [(i, to(i)) for i in range(2 * RING)]


ACROSS = [(i, i ^ RING) for i in range(2 * RING)]


def after(value, *done):
    return lax.optimization_barrier((value, *done))[0]


def along(value, distance, *done):
    return lax.ppermute(after(value, *done), "tile", shift(distance))


def across(value, *done):
    return lax.ppermute(after(value, *done), "tile", ACROSS)


def split(x):
    high = x.astype(BF16)
    return high, (x - high.astype(F32)).astype(BF16)


def dot(a, b, dims=(((1,), (0,)), ((), ()))):
    return lax.dot_general(a, b, dims, preferred_element_type=F32)


def split_dot(a, b, dims=(((1,), (0,)), ((), ()))):
    (ah, al), (bh, bl) = a, b
    return dot(ah, bh, dims) + dot(ah, bl, dims) + dot(al, bh, dims)


def running(mask):
    n = mask.shape[1]
    upper = lax.broadcasted_iota(I32, (n, n), 0) <= lax.broadcasted_iota(I32, (n, n), 1)
    ones = jnp.where(upper, 1.0, 0.0).astype(BF16)
    return dot(jnp.where(mask, 1.0, 0.0).astype(BF16), ones).astype(I32)


def pack_kernel(width, place_ref, lists_ref, *refs):
    uppers, outs, sel_ref = refs[:4], refs[4 : 4 + RING], refs[4 + RING]
    half, z = place_ref[0], place_ref[1]
    own = lists_ref[pl.ds(z, 1), :]
    count = own.shape[1]
    owner = lax.broadcast_in_dim(lax.div(own, width), (RING, count), (0, 1))
    target = lax.rem(lax.broadcasted_iota(I32, (RING, count), 0) + z, RING) + half * RING
    mask = owner == target
    rank = jnp.where(mask, running(mask) - 1, -1)
    slot = lax.broadcasted_iota(I32, (SLOT, count), 0)
    for d in range(RING):
        row = lax.broadcast_in_dim(rank[d : d + 1, :], (SLOT, count), (0, 1))
        sel_ref[d * SLOT : (d + 1) * SLOT, :] = jnp.where(row == slot, 1.0, 0.0).astype(BF16)
    parts = [split(ref[...]) for ref in uppers]
    high = jnp.concatenate([p[0] for p in parts], axis=1)
    low = jnp.concatenate([p[1] for p in parts], axis=1)
    packed = dot(sel_ref[...], high, TRANSPOSED) + dot(sel_ref[...], low, TRANSPOSED)
    for d in range(RING):
        outs[d][...] = packed[d * SLOT : (d + 1) * SLOT, :]


def factor_kernel(width, place_ref, lists_ref, *refs):
    blocks, refs = refs[:RING], refs[RING:]
    own_inv, refs = refs[:RING], refs[RING:]
    other_inv, refs = refs[:2], refs[2:]
    outs, (inv_ref, sel_ref, rank_ref) = refs[:4], refs[4:]
    half, z = place_ref[0], place_ref[1]
    me = half * RING + z
    lists = lists_ref[...]
    count = lists.shape[1]
    mask = lax.div(lists, width) == me
    rank_ref[...] = jnp.where(mask, running(mask) - 1, -1)
    per = count // 2
    rows = own_inv[0].shape[0] // 2

    def put(values, source_half, distance):
        at = (source_half * RING + lax.rem(z - distance + RING, RING)) * rows
        for child in range(2):
            inv_ref[child, pl.ds(pl.multiple_of(at, rows), rows), :] = values[child * rows : (child + 1) * rows]

    for k, distance in enumerate(INVERSE_ORDER):
        put(own_inv[k][...], half, distance)
        piece = other_inv[k // 4][(k % 4) * 2 * rows : (k % 4 + 1) * 2 * rows, :]
        put(piece, 1 - half, distance)
    slot = lax.broadcasted_iota(I32, (SLOT, per), 0)
    column = lax.broadcasted_iota(I32, (width, per), 0)
    for d in range(RING):
        source = lax.rem(z - d + RING, RING)
        index = lists_ref[pl.ds(source, 1), :] - me * width
        rank = rank_ref[pl.ds(source, 1), :]
        for child in range(2):
            cut = slice(child * per, (child + 1) * per)
            r = lax.broadcast_in_dim(rank[:, cut], (SLOT, per), (0, 1))
            c = lax.broadcast_in_dim(index[:, cut], (width, per), (0, 1))
            here = jnp.where(r == slot, 1.0, 0.0).astype(BF16)
            there = jnp.where(c == column, 1.0, 0.0).astype(BF16)
            sel_ref[child, d * SLOT : (d + 1) * SLOT, :] = dot(here, there, TRANSPOSED).astype(BF16)
    upper = split(jnp.concatenate([b[...] for b in blocks], axis=0))
    for child in range(2):
        factor = split_dot(split(inv_ref[child]), upper, TRANSPOSED)
        high, low = split(factor)
        outs[2 * child][...] = dot(high, sel_ref[child]).astype(BF16)
        outs[2 * child + 1][...] = dot(low, sel_ref[child]).astype(BF16)


INVERSE_ORDER = (0, 1, -1, 2, -2, 3, -3, 4)


def update_kernel(shards, place_ref, index_ref, acc_ref, *refs):
    lowers, refs = refs[: len(shards)], refs[len(shards) :]
    factors, (out_ref, upd_ref, sem) = refs[:4], refs[4:]
    half, z = place_ref[0], place_ref[1]
    copy = pltpu.make_async_copy(acc_ref, out_ref, sem)
    copy.start()
    rows = lowers[0].shape[0]
    for k, (child, own, distance) in enumerate(shards):
        lower = split(lowers[k][...])
        factor = (factors[2 * child][...], factors[2 * child + 1][...])
        upd_ref[k * rows : (k + 1) * rows, :] = split_dot(lower, factor)
    copy.wait()
    step = 16
    for k, (child, own, distance) in enumerate(shards):
        source_half = half if own else 1 - half
        base = child * 2 * RING * rows + (source_half * RING + lax.rem(z - distance + RING, RING)) * rows

        def body(i, _, k=k, base=base):
            at = [index_ref[base + i * step + j] for j in range(step)]
            upd = upd_ref[pl.ds(pl.multiple_of(k * rows + i * step, 8), step), :]
            old = [out_ref[pl.ds(a, 1), :] for a in at]
            new = [old[j] - upd[j : j + 1, :] for j in range(step)]
            for j in range(step):
                out_ref[pl.ds(at[j], 1), :] = new[j]
            return 0

        lax.fori_loop(0, rows // step, body, 0)


def vmem():
    return pl.BlockSpec(memory_space=pltpu.VMEM)


def smem():
    return pl.BlockSpec(memory_space=pltpu.SMEM)


def pack(width, place, lists, uppers):
    depth = uppers[0].shape[0]
    return pl.pallas_call(
        functools.partial(pack_kernel, width),
        out_shape=[jax.ShapeDtypeStruct((SLOT, depth), F32)] * RING,
        in_specs=[smem()] + [vmem()] * 5,
        out_specs=[vmem()] * RING,
        scratch_shapes=[pltpu.VMEM((RING * SLOT, lists.shape[1]), BF16)],
        compiler_params=pltpu.CompilerParams(vmem_limit_bytes=24 * MIB),
        cost_estimate=pl.CostEstimate(flops=2**29, bytes_accessed=2**21, transcendentals=0),
        name="pack",
    )(place, lists, *uppers)


def factor(width, place, lists, blocks, own_inv, other_inv):
    order = own_inv[0].shape[1]
    return pl.pallas_call(
        functools.partial(factor_kernel, width),
        out_shape=[jax.ShapeDtypeStruct((order, width), BF16)] * 4,
        in_specs=[smem()] + [vmem()] * (3 + 2 * RING),
        out_specs=[vmem()] * 4,
        scratch_shapes=[
            pltpu.VMEM((2, order, order), F32),
            pltpu.VMEM((2, RING * SLOT, width), BF16),
            pltpu.VMEM((RING, lists.shape[1]), I32),
        ],
        compiler_params=pltpu.CompilerParams(vmem_limit_bytes=32 * MIB),
        cost_estimate=pl.CostEstimate(flops=2**31, bytes_accessed=2**22, transcendentals=0),
        name="factor",
    )(place, lists, *blocks, *own_inv, *other_inv)


def subtract(place, index, acc, shards, lowers, factors):
    rows, width = lowers[0].shape[0], acc.shape[1]
    n = len(shards)
    return pl.pallas_call(
        functools.partial(update_kernel, tuple(shards)),
        out_shape=jax.ShapeDtypeStruct(acc.shape, F32),
        in_specs=[smem(), smem(), pl.BlockSpec(memory_space=pl.ANY)] + [vmem()] * (n + 4),
        out_specs=vmem(),
        scratch_shapes=[pltpu.VMEM((n * rows, width), F32), pltpu.SemaphoreType.DMA],
        compiler_params=pltpu.CompilerParams(vmem_limit_bytes=32 * MIB),
        cost_estimate=pl.CostEstimate(
            flops=n * rows * 512 * width * 6, bytes_accessed=2**23, transcendentals=0
        ),
        name="subtract",
    )(place, index, acc, *lowers, *factors)


def split_parts(matrix):
    high = matrix.astype(BF16)
    back = lax.optimization_barrier(high).astype(F32)
    return high, (matrix - back).astype(BF16)


def whole_factor(inverse_rows, upper, mapping, col_start, width):
    inverse = lax.all_gather(inverse_rows, "tile", axis=0, tiled=True)
    local = split_dot(split_parts(inverse), split_parts(upper))
    full = lax.all_gather(local, "tile", axis=1, tiled=True)
    high, low = split_parts(full)
    chosen = mapping[:, None] == col_start + jnp.arange(width, dtype=I32)[None, :]
    chosen = chosen.astype(BF16)
    return dot(high, chosen).astype(BF16), dot(low, chosen).astype(BF16)


def column_lists(first, second):
    lead = first.shape[:-1]
    parts = [
        jnp.swapaxes(m.reshape(*lead, 2, RING, -1), -3, -2).reshape(*lead, RING, -1)
        for m in (first, second)
    ]
    return jnp.concatenate(parts, axis=-1)


def shards(pivot_inverse, panel_upper, panel_lower, index_map, parent_base):
    base = parent_base[0]
    width = base.shape[1]
    tile = lax.axis_index("tile")
    group = lax.axis_index("front")
    half, z = tile // RING, tile % RING
    place = jnp.stack([half, z]).astype(I32)

    swap = [(i, i ^ 1) for i in range(lax.axis_size("front"))]
    u0, l0, i0 = panel_upper[0, 0], panel_lower[0, 0], pivot_inverse[0, 0]
    u1 = lax.ppermute(panel_upper[0, 1], "front", swap)
    l1 = lax.ppermute(panel_lower[0, 1], "front", swap)
    i1 = lax.ppermute(pivot_inverse[0, 1], "front", swap)

    firsts = index_map[:, 0]
    seconds = index_map.reshape(-1, 2, 2, index_map.shape[2])[:, ::-1, 1].reshape(firsts.shape)
    all_lists = column_lists(firsts, seconds)
    owners = all_lists // width
    per_pair = jnp.sum(
        (owners[:, :, None, :] == jnp.arange(2 * RING, dtype=I32)[None, None, :, None]).astype(F32), axis=-1
    )
    overflow = jnp.max(per_pair) > SLOT
    first = lax.dynamic_index_in_dim(firsts, group, 0, keepdims=False)
    second = lax.dynamic_index_in_dim(seconds, group, 0, keepdims=False)
    lists = lax.dynamic_index_in_dim(all_lists, group, 0, keepdims=False)
    index = jnp.concatenate([first, second])

    own = ({0: l0}, {0: l1})
    other = ({}, {})
    inv = {0: jnp.concatenate([i0, i1], axis=0)}

    def own_step(c, k, *done):
        own[c][k] = along(own[c][k - 1], 1, *done)
        own[c][-k] = along(own[c][1 - k], -1, *done)
        return own[c][k], own[c][-k]

    h1 = own_step(0, 1) + (across(u0),)
    h2 = own_step(1, 1) + (across(u1),)
    inv[1] = along(inv[0], 1)
    inv[-1] = along(inv[0], -1)
    h2 += (inv[1], inv[-1])
    h3 = own_step(0, 2, *h1)
    other[0][0] = across(l0, *h1)
    inv[2] = along(inv[1], 1, *h1)
    inv[-2] = along(inv[-1], -1, *h1)
    h3 += (other[0][0], inv[2], inv[-2])
    uppers = [u0, h1[2], u1, h2[2]]
    swapped = half == 0
    uppers = [
        jnp.where(swapped, uppers[0], uppers[1]),
        jnp.where(swapped, uppers[1], uppers[0]),
        jnp.where(swapped, uppers[2], uppers[3]),
        jnp.where(swapped, uppers[3], uppers[2]),
    ]
    packed = pack(width, place, lists, uppers)
    h4 = own_step(1, 2, *h2)
    other[1][0] = across(l1, *h2)
    inv[3] = along(inv[2], 1, *h2)
    inv[-3] = along(inv[-2], -1, *h2)
    h4 += (other[1][0], inv[3], inv[-3])
    blocks = {0: packed[0]}
    for d in (1, -1, 2, -2):
        blocks[d] = along(packed[d % RING], d, *h3)
    inv[4] = along(inv[3], 1, *h3)
    other[0][1] = across(own[0][1], *h3)
    other[1][1] = across(own[1][1], *h3)
    h5 = tuple(blocks[d] for d in (1, -1, 2, -2)) + (inv[4], other[0][1], other[1][1])
    h6 = own_step(0, 3, *h4)
    other[0][2] = across(own[0][2], *h4)
    inv_a = across(jnp.concatenate([inv[k] for k in INVERSE_ORDER[:4]], axis=0), *h4)
    h6 += (other[0][2], inv_a)
    for d in (3, -3, 4):
        blocks[d] = along(packed[d % RING], d, *h5)
    inv_b = across(jnp.concatenate([inv[k] for k in INVERSE_ORDER[4:]], axis=0), *h5)
    other[1][2] = across(own[1][2], *h5)
    h7 = (blocks[3], blocks[-3], blocks[4], inv_b, other[1][2])
    h8 = own_step(1, 3, *h6)
    other[0][-2] = across(own[0][-2], *h6)
    h8 += (other[0][-2],)
    late = [h7, h8]
    for c in range(2):
        other[c][3] = along(other[c][2], 1, *late[c])
        own[c][4] = along(own[c][-3], -1, *late[c])
        if c == 0:
            other[1][-2] = across(own[1][-2], *late[c])
            late.append((other[0][3], own[0][4], other[1][-2]))
        else:
            other[0][-1] = across(own[0][-1], *late[c])
            late.append((other[1][3], own[1][4], other[0][-1]))
    for c in range(2):
        other[c][4] = along(other[c][3], 1, *late[2 + c])
        other[c][-3] = along(other[c][-2], -1, *late[2 + c])
        if c == 0:
            other[1][-1] = across(own[1][-1], *late[2 + c])

    fast = factor(
        width,
        place,
        lists,
        [blocks[d if d <= 4 else d - RING] for d in range(RING)],
        [inv[k] for k in INVERSE_ORDER],
        [inv_a, inv_b],
    )

    def slow_way():
        start = tile * width
        return whole_factor(i0, u0, first, start, width) + whole_factor(i1, u1, second, start, width)

    factors = lax.cond(overflow, slow_way, lambda: tuple(fast))

    def take(acc, names):
        lowers = [(own if mine else other)[c][d] for c, mine, d in names]
        return subtract(place, index, acc, names, lowers, factors)

    acc = take(base, [(c, True, d) for c in range(2) for d in (0, 1, -1, 2, -2)])
    acc = take(acc, [(c, False, d) for c in range(2) for d in (0, 1, 2)] + [(c, True, d) for c in range(2) for d in (3, -3)])
    acc = take(acc, [(0, False, -2), (1, False, -2), (0, False, 3), (1, False, 3), (0, True, 4), (1, True, 4), (0, False, -1)])
    acc = take(acc, [(0, False, 4), (0, False, -3), (1, False, -1), (1, False, 4), (1, False, -3)])
    return acc[None]


def solution(mesh):
    return jax.shard_map(
        shards,
        mesh=mesh,
        in_specs=(
            P("front", None, "tile", None),
            P("front", None, None, "tile"),
            P("front", None, "tile", None),
            P(),
            P("front", None, "tile"),
        ),
        out_specs=P("front", None, "tile"),
        check_vma=False,
    )
```

```python
import functools

import jax
import jax.numpy as jnp
from jax import lax
from jax.experimental import pallas as pl
from jax.experimental.pallas import tpu as pltpu
from jax.sharding import PartitionSpec as P

RING = 8
SLOT = 64
MIB = 1024 * 1024
F32, BF16, I32 = jnp.float32, jnp.bfloat16, jnp.int32
TRANSPOSED = (((1,), (1,)), ((), ()))


def shift(distance):
    def to(i):
        return (i // RING) * RING + (i + distance) % RING

    return [(i, to(i)) for i in range(2 * RING)]


ACROSS = [(i, i ^ RING) for i in range(2 * RING)]


def after(value, *done):
    return lax.optimization_barrier((value, *done))[0]


def along(value, distance, *done):
    return lax.ppermute(after(value, *done), "tile", shift(distance))


def across(value, *done):
    return lax.ppermute(after(value, *done), "tile", ACROSS)


def split(x):
    high = x.astype(BF16)
    return high, (x - high.astype(F32)).astype(BF16)


def dot(a, b, dims=(((1,), (0,)), ((), ()))):
    return lax.dot_general(a, b, dims, preferred_element_type=F32)


def split_dot(a, b, dims=(((1,), (0,)), ((), ()))):
    (ah, al), (bh, bl) = a, b
    return dot(ah, bh, dims) + dot(ah, bl, dims) + dot(al, bh, dims)


def quotient(x, divisor):
    assert divisor & (divisor - 1) == 0
    return lax.shift_right_logical(x, jnp.full(x.shape, divisor.bit_length() - 1, x.dtype))


def running(mask):
    n = mask.shape[1]
    upper = lax.broadcasted_iota(I32, (n, n), 0) <= lax.broadcasted_iota(I32, (n, n), 1)
    ones = jnp.where(upper, 1.0, 0.0).astype(BF16)
    return dot(jnp.where(mask, 1.0, 0.0).astype(BF16), ones).astype(I32)


def fill_lists(place_ref, index_ref, lists_ref):
    half, group = place_ref[0], place_ref[2]
    per = lists_ref.shape[1] // 4
    for child, g in ((0, group), (1, jnp.bitwise_xor(group, 1))):
        for k, h in ((0, half), (1, 1 - half)):
            start = pl.multiple_of(h * RING * per, RING * per)
            row = index_ref[pl.ds(g, 1), child, pl.ds(start, RING * per)]
            at = (2 * child + k) * per
            for source in range(RING):
                lists_ref[source : source + 1, at : at + per] = row[:, source * per : (source + 1) * per]


def pack_kernel(width, place_ref, index_ref, *refs):
    uppers, outs, (lists_ref, sel_ref) = refs[:4], refs[4 : 4 + RING], refs[4 + RING :]
    half, z = place_ref[0], place_ref[1]
    fill_lists(place_ref, index_ref, lists_ref)
    own = lists_ref[pl.ds(z, 1), :]
    shape = (RING, own.shape[1])
    owner = lax.broadcast_in_dim(quotient(own, width), shape, (0, 1))
    target = ((lax.broadcasted_iota(I32, shape, 0) + z) & (RING - 1)) + half * RING
    mask = owner == target
    rank = jnp.where(mask, running(mask) - 1, -1)
    slot = lax.broadcasted_iota(I32, (SLOT, shape[1]), 0)
    for d in range(RING):
        row = lax.broadcast_in_dim(rank[d : d + 1, :], slot.shape, (0, 1))
        sel_ref[d * SLOT : (d + 1) * SLOT, :] = jnp.where(row == slot, 1.0, 0.0).astype(BF16)
    parts = [split(ref[...]) for ref in uppers]
    high = jnp.concatenate([p[0] for p in parts], axis=1)
    low = jnp.concatenate([p[1] for p in parts], axis=1)
    packed = dot(sel_ref[...], high, TRANSPOSED) + dot(sel_ref[...], low, TRANSPOSED)
    for d in range(RING):
        outs[d][...] = packed[d * SLOT : (d + 1) * SLOT, :]


def choose_kernel(width, place_ref, index_ref, sel_ref, most_ref, lists_ref, rank_ref):
    half, z = place_ref[0], place_ref[1]
    me = half * RING + z
    fill_lists(place_ref, index_ref, lists_ref)
    owner = quotient(lists_ref[...], width)
    counts = [jnp.sum(jnp.where(owner == t, 1.0, 0.0), axis=1, keepdims=True) for t in range(2 * RING)]
    most_ref[0] = jnp.max(functools.reduce(jnp.maximum, counts))
    mask = owner == me
    rank_ref[...] = jnp.where(mask, running(mask) - 1, -1)
    per = owner.shape[1] // 2
    slot = lax.broadcasted_iota(I32, (SLOT, per), 0)
    column = lax.broadcasted_iota(I32, (width, per), 0)
    for d in range(RING):
        source = (z - d) & (RING - 1)
        index = lists_ref[pl.ds(source, 1), :] - me * width
        rank = rank_ref[pl.ds(source, 1), :]
        for child in range(2):
            cut = slice(child * per, (child + 1) * per)
            r = lax.broadcast_in_dim(rank[:, cut], slot.shape, (0, 1))
            c = lax.broadcast_in_dim(index[:, cut], column.shape, (0, 1))
            here = jnp.where(r == slot, 1.0, 0.0).astype(BF16)
            there = jnp.where(c == column, 1.0, 0.0).astype(BF16)
            sel_ref[child, d * SLOT : (d + 1) * SLOT, :] = dot(here, there, TRANSPOSED).astype(BF16)


ORDER = [(own, d) for own in (True, False) for d in (0, 1, -1, 2, -2, 3, -3, 4)]
CHUNK = 512


def tile_of(place_ref, own, distance):
    half, z = place_ref[0], place_ref[1]
    return (half if own else 1 - half) * RING + ((z - distance) & (RING - 1))


def finish_kernel(place_ref, index_ref, most_ref, sel_ref, base_ref, *refs):
    slow, refs = refs[:4], refs[4:]
    blocks, panels, out_ref, refs = refs[:RING], refs[RING : 3 * RING], refs[3 * RING], refs[3 * RING + 1 :]
    lower_ref, upper_ref, inv_ref, factor_ref, upd_ref, sems = refs
    rows = lower_ref.shape[1] // (2 * RING)
    order = inv_ref.shape[1]
    part = order // (2 * RING)
    copies = []

    def begin(source, target):
        copy = pltpu.make_async_copy(source, target, sems.at[len(copies)])
        copy.start()
        copies.append(copy)

    for d in range(RING):
        begin(blocks[d], upper_ref.at[pl.ds(d * SLOT, SLOT)])
    for panel, (own, distance) in zip(panels, ORDER):
        at = pl.multiple_of(tile_of(place_ref, own, distance) * part, part)
        for child in range(2):
            begin(panel.at[pl.ds(2 * rows + child * part, part)], inv_ref.at[child, pl.ds(at, part)])
    ready = len(copies)
    for child in range(2):
        for k in range(2 * RING):
            begin(panels[k].at[pl.ds(child * rows, rows)], lower_ref.at[child, pl.ds(k * rows, rows)])
    begin(base_ref, out_ref)
    for copy in copies[:ready]:
        copy.wait()
    upper = split(upper_ref[...])
    for child in range(2):
        high, low = split(split_dot(split(inv_ref[child]), upper, TRANSPOSED))
        factor_ref[2 * child] = dot(high, sel_ref[child]).astype(BF16)
        factor_ref[2 * child + 1] = dot(low, sel_ref[child]).astype(BF16)

    @pl.when(most_ref[0] > SLOT)
    def _():
        for k in range(4):
            pltpu.sync_copy(slow[k], factor_ref.at[k])

    step = 16
    waits = iter(copies[ready:-1])
    for child in range(2):
        factor = (factor_ref[2 * child], factor_ref[2 * child + 1])
        for start in range(0, lower_ref.shape[1], CHUNK):
            for _ in range(CHUNK // rows):
                next(waits).wait()
            lower = split(lower_ref[child, start : start + CHUNK, :])
            upd_ref[start : start + CHUNK, :] = split_dot(lower, factor)
        if child == 0:
            copies[-1].wait()
        for k, (own, distance) in enumerate(ORDER):
            base = (child * 2 * RING + tile_of(place_ref, own, distance)) * rows

            def body(i, _, k=k, base=base):
                to = [index_ref[base + i * step + j] for j in range(step)]
                upd = upd_ref[pl.ds(pl.multiple_of(k * rows + i * step, 8), step), :]
                old = [out_ref[pl.ds(a, 1), :] for a in to]
                new = [old[j] - upd[j : j + 1, :] for j in range(step)]
                for j in range(step):
                    out_ref[pl.ds(to[j], 1), :] = new[j]
                return 0

            lax.fori_loop(0, rows // step, body, 0)


def vmem():
    return pl.BlockSpec(memory_space=pltpu.VMEM)


def smem():
    return pl.BlockSpec(memory_space=pltpu.SMEM)


def pack(width, place, index_map, uppers):
    depth, per = uppers[0].shape
    return pl.pallas_call(
        functools.partial(pack_kernel, width),
        out_shape=[jax.ShapeDtypeStruct((SLOT, depth), F32)] * RING,
        in_specs=[smem()] + [vmem()] * 5,
        out_specs=[vmem()] * RING,
        scratch_shapes=[pltpu.VMEM((RING, 4 * per), I32), pltpu.VMEM((RING * SLOT, 4 * per), BF16)],
        compiler_params=pltpu.CompilerParams(vmem_limit_bytes=14 * MIB),
        cost_estimate=pl.CostEstimate(flops=2**30, bytes_accessed=2**21, transcendentals=0),
        name="pack",
    )(place, index_map, *uppers)


def choose(width, place, index_map):
    per = index_map.shape[2] // (2 * RING)
    return pl.pallas_call(
        functools.partial(choose_kernel, width),
        out_shape=[jax.ShapeDtypeStruct((2, RING * SLOT, width), BF16), jax.ShapeDtypeStruct((1,), F32)],
        in_specs=[smem(), vmem()],
        out_specs=[vmem(), smem()],
        scratch_shapes=[pltpu.VMEM((RING, 4 * per), I32), pltpu.VMEM((RING, 4 * per), I32)],
        compiler_params=pltpu.CompilerParams(vmem_limit_bytes=14 * MIB),
        cost_estimate=pl.CostEstimate(flops=2**30, bytes_accessed=2**21, transcendentals=0),
        name="choose",
    )(place, index_map)


def finish(place, index, most, sel, base, slow, blocks, panels):
    width, order, count = base.shape[1], panels[0].shape[1], index.shape[0] // 2
    anywhere = pl.BlockSpec(memory_space=pl.ANY)
    return pl.pallas_call(
        finish_kernel,
        out_shape=jax.ShapeDtypeStruct(base.shape, F32),
        in_specs=[smem()] * 3 + [vmem()] + [anywhere] * (5 + 3 * RING),
        out_specs=vmem(),
        scratch_shapes=[
            pltpu.VMEM((2, count, order), F32),
            pltpu.VMEM((RING * SLOT, order), F32),
            pltpu.VMEM((2, order, order), F32),
            pltpu.VMEM((4, order, width), BF16),
            pltpu.VMEM((count, width), F32),
            pltpu.SemaphoreType.DMA((RING + 8 * RING + 1,)),
        ],
        compiler_params=pltpu.CompilerParams(vmem_limit_bytes=VMEM_MIB * MIB),
        cost_estimate=pl.CostEstimate(flops=2**33, bytes_accessed=2**24, transcendentals=0),
        name="finish",
    )(place, index, most, sel, base, *slow, *blocks, *panels)


VMEM_MIB = 34


def split_parts(matrix):
    high = matrix.astype(BF16)
    back = lax.optimization_barrier(high).astype(F32)
    return high, (matrix - back).astype(BF16)


def gather(x, axis):
    n = lax.axis_size("tile")
    tile = lax.axis_index("tile")
    size = x.shape[axis]
    whole = jnp.zeros(tuple(n * m if a == axis else m for a, m in enumerate(x.shape)), x.dtype)

    def body(k, state):
        whole, x = state
        whole = lax.dynamic_update_slice_in_dim(whole, x, ((tile - k) % n) * size, axis)
        return whole, lax.ppermute(x, "tile", [(i, (i + 1) % n) for i in range(n)])

    return lax.fori_loop(0, n, body, (whole, x))[0]


def whole_factor(inverse_rows, upper, mapping, col_start, width):
    inverse = gather(inverse_rows, 0)
    full = gather(split_dot(split_parts(inverse), split_parts(upper)), 1)
    high, low = split_parts(full)
    chosen = mapping[:, None] == col_start + jnp.arange(width, dtype=I32)[None, :]
    chosen = chosen.astype(BF16)
    return dot(high, chosen).astype(BF16), dot(low, chosen).astype(BF16)


def shards(pivot_inverse, panel_upper, panel_lower, index_map, parent_base):
    base = parent_base[0]
    width = base.shape[1]
    tile = lax.axis_index("tile")
    group = lax.axis_index("front")
    half, z = tile // RING, tile % RING
    place = jnp.stack([half, z, group]).astype(I32)

    swap = [(i, i ^ 1) for i in range(lax.axis_size("front"))]
    u0, l0, i0 = panel_upper[0, 0], panel_lower[0, 0], pivot_inverse[0, 0]
    i1 = lax.ppermute(pivot_inverse[0, 1], "front", swap)
    l1 = lax.ppermute(panel_lower[0, 1], "front", swap)
    u1 = lax.ppermute(panel_upper[0, 1], "front", swap)
    first = lax.dynamic_index_in_dim(index_map[:, 0], group, 0, keepdims=False)
    second = lax.dynamic_index_in_dim(index_map[:, 1], group ^ 1, 0, keepdims=False)
    index = jnp.concatenate([first, second])

    own, other = {0: jnp.concatenate([l0, l1, i0, i1], axis=0)}, {}
    far0, far1 = across(u0), across(u1)
    own[1], own[-1] = along(own[0], 1), along(own[0], -1)
    packed = pack(width, place, index_map, [u0, far0, u1, far1])
    blocks = {0: packed[0]}
    sel, most = choose(width, place, index_map)

    def slow_way():
        start = tile * width
        return whole_factor(i0, u0, first, start, width) + whole_factor(i1, u1, second, start, width)

    def fast_way():
        return (jnp.zeros((l0.shape[1], width), BF16),) * 4

    slow = lax.cond(most[0] > SLOT, slow_way, fast_way)

    def send_block(d, *done):
        blocks[d] = along(packed[d % RING], d, *done)

    other[0] = across(own[0], far0)
    own[2], own[-2] = along(own[1], 1), along(own[-1], -1)
    send_block(1)
    send_block(-1)
    send_block(4, own[1])
    send_block(-2, own[-1])
    other[2] = across(own[2], far1)
    own[3], own[-3] = along(own[2], 1, slow[0]), along(own[-2], -1)
    send_block(2, own[2])
    send_block(-3, own[-2])
    other[-2] = across(own[-2], other[0])
    other[3] = along(other[2], 1)
    own[4] = along(own[-3], -1)
    send_block(3, own[3])
    other[1] = across(own[1], other[2])
    other[4], other[-3] = along(other[3], 1), along(other[-2], -1, own[-3])
    other[-1] = across(own[-1], other[-2])

    panels = [(own if mine else other)[d] for mine, d in ORDER]
    arrived = [blocks[d if d <= 4 else d - RING] for d in range(RING)]
    return finish(place, index, most, sel, base, slow, arrived, panels)[None]


def solution(mesh):
    return jax.shard_map(
        shards,
        mesh=mesh,
        in_specs=(
            P("front", None, "tile", None),
            P("front", None, None, "tile"),
            P("front", None, "tile", None),
            P(),
            P("front", None, "tile"),
        ),
        out_specs=P("front", None, "tile"),
        check_vma=False,
    )
```

```python
import functools

import jax
import jax.numpy as jnp
from jax import lax
from jax.experimental import pallas as pl
from jax.experimental.pallas import tpu as pltpu
from jax.sharding import PartitionSpec as P

RING = 8
SLOT = 64
MIB = 1024 * 1024
F32, BF16, I32 = jnp.float32, jnp.bfloat16, jnp.int32
TRANSPOSED = (((1,), (1,)), ((), ()))


def shift(distance):
    def to(i):
        return (i // RING) * RING + (i + distance) % RING

    return [(i, to(i)) for i in range(2 * RING)]


ACROSS = [(i, i ^ RING) for i in range(2 * RING)]


def after(value, *done):
    return lax.optimization_barrier((value, *done))[0]


def along(value, distance, *done):
    return lax.ppermute(after(value, *done), "tile", shift(distance))


def across(value, *done):
    return lax.ppermute(after(value, *done), "tile", ACROSS)


def split(x):
    high = x.astype(BF16)
    return high, (x - high.astype(F32)).astype(BF16)


def dot(a, b, dims=(((1,), (0,)), ((), ()))):
    return lax.dot_general(a, b, dims, preferred_element_type=F32)


def split_dot(a, b, dims=(((1,), (0,)), ((), ()))):
    (ah, al), (bh, bl) = a, b
    return dot(ah, bh, dims) + dot(ah, bl, dims) + dot(al, bh, dims)


def quotient(x, divisor):
    assert divisor & (divisor - 1) == 0
    return lax.shift_right_logical(x, jnp.full(x.shape, divisor.bit_length() - 1, x.dtype))


def running(mask):
    n = mask.shape[1]
    upper = lax.broadcasted_iota(I32, (n, n), 0) <= lax.broadcasted_iota(I32, (n, n), 1)
    ones = jnp.where(upper, 1.0, 0.0).astype(BF16)
    return dot(jnp.where(mask, 1.0, 0.0).astype(BF16), ones).astype(I32)


def fill_lists(place_ref, index_ref, lists_ref):
    half, group = place_ref[0], place_ref[2]
    per = lists_ref.shape[1] // 4
    for child, g in ((0, group), (1, jnp.bitwise_xor(group, 1))):
        for k, h in ((0, half), (1, 1 - half)):
            start = pl.multiple_of(h * RING * per, RING * per)
            row = index_ref[pl.ds(g, 1), child, pl.ds(start, RING * per)]
            at = (2 * child + k) * per
            for source in range(RING):
                lists_ref[source : source + 1, at : at + per] = row[:, source * per : (source + 1) * per]


def pack_kernel(width, place_ref, index_ref, *refs):
    uppers, outs, (lists_ref, sel_ref) = refs[:4], refs[4 : 4 + RING], refs[4 + RING :]
    half, z = place_ref[0], place_ref[1]
    fill_lists(place_ref, index_ref, lists_ref)
    own = lists_ref[pl.ds(z, 1), :]
    shape = (RING, own.shape[1])
    owner = lax.broadcast_in_dim(quotient(own, width), shape, (0, 1))
    target = ((lax.broadcasted_iota(I32, shape, 0) + z) & (RING - 1)) + half * RING
    mask = owner == target
    rank = jnp.where(mask, running(mask) - 1, -1)
    slot = lax.broadcasted_iota(I32, (SLOT, shape[1]), 0)
    for d in range(RING):
        row = lax.broadcast_in_dim(rank[d : d + 1, :], slot.shape, (0, 1))
        sel_ref[d * SLOT : (d + 1) * SLOT, :] = jnp.where(row == slot, 1.0, 0.0).astype(BF16)
    parts = [split(ref[...]) for ref in uppers]
    high = jnp.concatenate([p[0] for p in parts], axis=1)
    low = jnp.concatenate([p[1] for p in parts], axis=1)
    packed = dot(sel_ref[...], high, TRANSPOSED) + dot(sel_ref[...], low, TRANSPOSED)
    for d in range(RING):
        outs[d][...] = packed[d * SLOT : (d + 1) * SLOT, :]


def choose_kernel(width, place_ref, index_ref, sel_ref, most_ref, lists_ref, rank_ref):
    half, z = place_ref[0], place_ref[1]
    me = half * RING + z
    fill_lists(place_ref, index_ref, lists_ref)
    owner = quotient(lists_ref[...], width)
    counts = [jnp.sum(jnp.where(owner == t, 1.0, 0.0), axis=1, keepdims=True) for t in range(2 * RING)]
    most_ref[0] = jnp.max(functools.reduce(jnp.maximum, counts))
    mask = owner == me
    rank_ref[...] = jnp.where(mask, running(mask) - 1, -1)
    per = owner.shape[1] // 2
    slot = lax.broadcasted_iota(I32, (SLOT, per), 0)
    column = lax.broadcasted_iota(I32, (width, per), 0)
    for d in range(RING):
        source = (z - d) & (RING - 1)
        index = lists_ref[pl.ds(source, 1), :] - me * width
        rank = rank_ref[pl.ds(source, 1), :]
        for child in range(2):
            cut = slice(child * per, (child + 1) * per)
            r = lax.broadcast_in_dim(rank[:, cut], slot.shape, (0, 1))
            c = lax.broadcast_in_dim(index[:, cut], column.shape, (0, 1))
            here = jnp.where(r == slot, 1.0, 0.0).astype(BF16)
            there = jnp.where(c == column, 1.0, 0.0).astype(BF16)
            sel_ref[child, d * SLOT : (d + 1) * SLOT, :] = dot(here, there, TRANSPOSED).astype(BF16)


ORDER = [(own, d) for own in (True, False) for d in (0, 1, -1, 2, -2, 3, -3, 4)]
CHUNK = 1024


def tile_of(place_ref, own, distance):
    half, z = place_ref[0], place_ref[1]
    return (half if own else 1 - half) * RING + ((z - distance) & (RING - 1))


LANES = 128


def load_kernel(base_ref, out_ref):
    for h in range(out_ref.shape[1]):
        out_ref[:, h, :] = base_ref[:, h * LANES : (h + 1) * LANES]


def finish_kernel(where, place_ref, index_ref, most_ref, sel_ref, acc_in_ref, *refs):
    slow, refs = refs[:4], refs[4:]
    first_ref, panels, refs = refs[0], refs[1 : 1 + 2 * RING], refs[1 + 2 * RING :]
    out_ref, acc_ref, high_ref, low_ref, inv_ref, factor_ref, upd_ref = refs
    count, order = high_ref.shape
    rows, part = count // (2 * RING), order // (2 * RING)
    halves = acc_ref.shape[1]
    for panel, (own, distance) in zip(panels, ORDER):
        at = pl.multiple_of(tile_of(place_ref, own, distance) * part, part)
        for child in range(2):
            start = 2 * rows + child * part
            inv_ref[child, pl.ds(at, part), :] = panel[start : start + part, :]
    arrived = [first_ref[...]]
    for d in range(1, RING):
        arrived += [panels[k][start : start + size, :] for k, start, size in where[d]]
    upper = split(jnp.concatenate(arrived, axis=0))
    for child in range(2):
        high, low = split(split_dot(split(inv_ref[child]), upper, TRANSPOSED))
        factor_ref[2 * child] = dot(high, sel_ref[child]).astype(BF16)
        factor_ref[2 * child + 1] = dot(low, sel_ref[child]).astype(BF16)

    @pl.when(most_ref[0] > SLOT)
    def _():
        for k in range(4):
            pltpu.sync_copy(slow[k], factor_ref.at[k])

    step = 16
    for child in range(2):
        for k in range(2 * RING):
            high, low = split(panels[k][child * rows : (child + 1) * rows, :])
            high_ref[k * rows : (k + 1) * rows, :] = high
            low_ref[k * rows : (k + 1) * rows, :] = low
        factor = (factor_ref[2 * child], factor_ref[2 * child + 1])
        for start in range(0, count, CHUNK):
            cut = slice(start, start + CHUNK)
            upd = split_dot((high_ref[cut, :], low_ref[cut, :]), factor)
            for h in range(halves):
                upd_ref[cut, h, :] = upd[:, h * LANES : (h + 1) * LANES]
        for k, (own, distance) in enumerate(ORDER):
            base = (child * 2 * RING + tile_of(place_ref, own, distance)) * rows

            def body(i, _, k=k, base=base):
                to = [index_ref[base + i * step + j] for j in range(step)]
                at = k * rows + i * step
                new = [acc_ref[to[j]] - upd_ref[at + j] for j in range(step)]
                for j in range(step):
                    acc_ref[to[j]] = new[j]
                return 0

            lax.fori_loop(0, rows // step, body, 0)
    for h in range(halves):
        out_ref[:, h * LANES : (h + 1) * LANES] = acc_ref[:, h, :]


def vmem():
    return pl.BlockSpec(memory_space=pltpu.VMEM)


def smem():
    return pl.BlockSpec(memory_space=pltpu.SMEM)


def pack(width, place, index_map, uppers):
    depth, per = uppers[0].shape
    return pl.pallas_call(
        functools.partial(pack_kernel, width),
        out_shape=[jax.ShapeDtypeStruct((SLOT, depth), F32)] * RING,
        in_specs=[smem()] + [vmem()] * 5,
        out_specs=[vmem()] * RING,
        scratch_shapes=[pltpu.VMEM((RING, 4 * per), I32), pltpu.VMEM((RING * SLOT, 4 * per), BF16)],
        compiler_params=pltpu.CompilerParams(vmem_limit_bytes=14 * MIB),
        cost_estimate=pl.CostEstimate(flops=2**30, bytes_accessed=2**21, transcendentals=0),
        name="pack",
    )(place, index_map, *uppers)


def choose(width, place, index_map):
    per = index_map.shape[2] // (2 * RING)
    return pl.pallas_call(
        functools.partial(choose_kernel, width),
        out_shape=[jax.ShapeDtypeStruct((2, RING * SLOT, width), BF16), jax.ShapeDtypeStruct((1,), F32)],
        in_specs=[smem(), vmem()],
        out_specs=[vmem(), smem()],
        scratch_shapes=[pltpu.VMEM((RING, 4 * per), I32), pltpu.VMEM((RING, 4 * per), I32)],
        compiler_params=pltpu.CompilerParams(vmem_limit_bytes=14 * MIB),
        cost_estimate=pl.CostEstimate(flops=2**30, bytes_accessed=2**21, transcendentals=0),
        name="choose",
    )(place, index_map)


def load(base):
    return pl.pallas_call(
        load_kernel,
        out_shape=jax.ShapeDtypeStruct((base.shape[0], base.shape[1] // LANES, LANES), F32),
        in_specs=[vmem()],
        out_specs=vmem(),
        compiler_params=pltpu.CompilerParams(vmem_limit_bytes=12 * MIB),
        cost_estimate=pl.CostEstimate(flops=0, bytes_accessed=2**23, transcendentals=0),
        name="load",
    )(base)


def finish(place, index, most, sel, acc, slow, first, panels, where):
    order, count = panels[0].shape[1], index.shape[0] // 2
    width = acc.shape[1] * acc.shape[2]
    return pl.pallas_call(
        functools.partial(finish_kernel, where),
        out_shape=[jax.ShapeDtypeStruct((acc.shape[0], width), F32), jax.ShapeDtypeStruct(acc.shape, F32)],
        in_specs=[smem()] * 3 + [vmem()] * 2 + [pl.BlockSpec(memory_space=pl.ANY)] * 4 + [vmem()] * (1 + 2 * RING),
        out_specs=[vmem()] * 2,
        input_output_aliases={4: 1},
        scratch_shapes=[
            pltpu.VMEM((count, order), BF16),
            pltpu.VMEM((count, order), BF16),
            pltpu.VMEM((2, order, order), F32),
            pltpu.VMEM((4, order, width), BF16),
            pltpu.VMEM((count, *acc.shape[1:]), F32),
        ],
        compiler_params=pltpu.CompilerParams(vmem_limit_bytes=28 * MIB),
        cost_estimate=pl.CostEstimate(flops=2**33, bytes_accessed=2**24, transcendentals=0),
        name="finish",
    )(place, index, most, sel, acc, *slow, first, *panels)[0]


def split_parts(matrix):
    high = matrix.astype(BF16)
    back = lax.optimization_barrier(high).astype(F32)
    return high, (matrix - back).astype(BF16)


def gather(x, axis):
    n = lax.axis_size("tile")
    tile = lax.axis_index("tile")
    size = x.shape[axis]
    whole = jnp.zeros(tuple(n * m if a == axis else m for a, m in enumerate(x.shape)), x.dtype)

    def body(k, state):
        whole, x = state
        whole = lax.dynamic_update_slice_in_dim(whole, x, ((tile - k) % n) * size, axis)
        return whole, lax.ppermute(x, "tile", [(i, (i + 1) % n) for i in range(n)])

    return lax.fori_loop(0, n, body, (whole, x))[0]


def whole_factor(inverse_rows, upper, mapping, col_start, width):
    inverse = gather(inverse_rows, 0)
    full = gather(split_dot(split_parts(inverse), split_parts(upper)), 1)
    high, low = split_parts(full)
    chosen = mapping[:, None] == col_start + jnp.arange(width, dtype=I32)[None, :]
    chosen = chosen.astype(BF16)
    return dot(high, chosen).astype(BF16), dot(low, chosen).astype(BF16)


def shards(pivot_inverse, panel_upper, panel_lower, index_map, parent_base):
    base = parent_base[0]
    width = base.shape[1]
    tile = lax.axis_index("tile")
    group = lax.axis_index("front")
    half, z = tile // RING, tile % RING
    place = jnp.stack([half, z, group]).astype(I32)

    swap = [(i, i ^ 1) for i in range(lax.axis_size("front"))]
    u0, l0, i0 = panel_upper[0, 0], panel_lower[0, 0], pivot_inverse[0, 0]
    i1 = lax.ppermute(pivot_inverse[0, 1], "front", swap)
    l1 = lax.ppermute(panel_lower[0, 1], "front", swap)
    u1 = lax.ppermute(panel_upper[0, 1], "front", swap)
    first = lax.dynamic_index_in_dim(index_map[:, 0], group, 0, keepdims=False)
    second = lax.dynamic_index_in_dim(index_map[:, 1], group ^ 1, 0, keepdims=False)
    index = jnp.concatenate([first, second])

    own, other = {0: jnp.concatenate([l0, l1, i0, i1], axis=0)}, {}
    far0, far1 = across(u0), across(u1)
    own[1], own[-1] = along(own[0], 1), along(own[0], -1)
    sel, most = choose(width, place, index_map)

    def slow_way():
        start = tile * width
        return whole_factor(i0, u0, first, start, width) + whole_factor(i1, u1, second, start, width)

    def fast_way():
        return (jnp.zeros((l0.shape[1], width), BF16),) * 4

    slow = lax.cond(most[0] > SLOT, slow_way, fast_way)
    packed = pack(width, after(place, slow[0]), index_map, [u0, far0, u1, far1])
    acc = load(after(base, packed[1]))

    size, part = own[0].shape[0], SLOT // 2

    def passed_on(x):
        return x[: x.shape[0] - SLOT]

    up = jnp.concatenate([own[1], packed[4][:part], packed[3], packed[2], packed[1]], axis=0)
    down = jnp.concatenate([own[-1], packed[4][part:], packed[5], packed[6], packed[7]], axis=0)
    own[2], own[-2] = along(up, 1), along(down, -1)
    other[0] = across(own[0], far0, packed[1])
    done = own[2], own[-2]
    own[3], own[-3] = along(passed_on(own[2]), 1), along(passed_on(own[-2]), -1)
    other[2] = across(own[2][:size], *done)
    done = own[3], own[-3], other[0]
    other[-2] = across(own[-2][:size], *done)
    own[4] = along(passed_on(own[-3]), -1, *done)
    other[3] = along(jnp.concatenate([other[2], own[3][size : size + part + SLOT]], axis=0), 1, *done)
    done = own[4], other[3], other[2]
    other[1] = across(own[1], *done)
    other[4] = along(passed_on(other[3]), 1, *done)
    other[-3] = along(jnp.concatenate([other[-2], own[4][size : size + part]], axis=0), -1, *done)
    other[-1] = across(own[-1], other[-2], *done)

    panels = [(own if mine else other)[d] for mine, d in ORDER]
    place_of = {x: k for k, x in enumerate(ORDER)}
    near = {1: (True, 2), 2: (True, 3), 3: (False, 3), 7: (True, -2), 6: (True, -3), 5: (True, 4)}
    where = {}
    for d, x in near.items():
        rows = panels[place_of[x]].shape[0]
        where[d] = [(place_of[x], rows - SLOT, SLOT)]
    where[4] = [(place_of[x], size, part) for x in ((False, 4), (False, -3))]
    return finish(place, index, most, sel, acc, slow, packed[0], panels, where)[None]


def solution(mesh):
    return jax.shard_map(
        shards,
        mesh=mesh,
        in_specs=(
            P("front", None, "tile", None),
            P("front", None, None, "tile"),
            P("front", None, "tile", None),
            P(),
            P("front", None, "tile"),
        ),
        out_specs=P("front", None, "tile"),
        check_vma=False,
    )
```

```python
import functools

import jax
import jax.numpy as jnp
from jax import lax
from jax.experimental import pallas as pl
from jax.experimental.pallas import tpu as pltpu
from jax.sharding import PartitionSpec as P

RING = 8
SLOT = 64
MIB = 1024 * 1024
F32, BF16, I32 = jnp.float32, jnp.bfloat16, jnp.int32
TRANSPOSED = (((1,), (1,)), ((), ()))


def shift(distance):
    def to(i):
        return (i // RING) * RING + (i + distance) % RING

    return [(i, to(i)) for i in range(2 * RING)]


ACROSS = [(i, i ^ RING) for i in range(2 * RING)]


def after(value, *done):
    return lax.optimization_barrier((value, *done))[0]


def along(value, distance, *done):
    return lax.ppermute(after(value, *done), "tile", shift(distance))


def across(value, *done):
    return lax.ppermute(after(value, *done), "tile", ACROSS)


def split(x):
    high = x.astype(BF16)
    return high, (x - high.astype(F32)).astype(BF16)


def dot(a, b, dims=(((1,), (0,)), ((), ()))):
    return lax.dot_general(a, b, dims, preferred_element_type=F32)


def split_dot(a, b, dims=(((1,), (0,)), ((), ()))):
    (ah, al), (bh, bl) = a, b
    return dot(ah, bh, dims) + dot(ah, bl, dims) + dot(al, bh, dims)


def quotient(x, divisor):
    assert divisor & (divisor - 1) == 0
    return lax.shift_right_logical(x, jnp.full(x.shape, divisor.bit_length() - 1, x.dtype))


def running(mask):
    n = mask.shape[1]
    upper = lax.broadcasted_iota(I32, (n, n), 0) <= lax.broadcasted_iota(I32, (n, n), 1)
    ones = jnp.where(upper, 1.0, 0.0).astype(BF16)
    return dot(jnp.where(mask, 1.0, 0.0).astype(BF16), ones).astype(I32)


def fill_lists(place_ref, index_ref, lists_ref):
    half, group = place_ref[0], place_ref[2]
    per = lists_ref.shape[1] // 4
    for child, g in ((0, group), (1, jnp.bitwise_xor(group, 1))):
        for k, h in ((0, half), (1, 1 - half)):
            start = pl.multiple_of(h * RING * per, RING * per)
            row = index_ref[pl.ds(g, 1), child, pl.ds(start, RING * per)]
            at = (2 * child + k) * per
            for source in range(RING):
                lists_ref[source : source + 1, at : at + per] = row[:, source * per : (source + 1) * per]


def pack_kernel(width, place_ref, index_ref, *refs):
    uppers, outs, (lists_ref, sel_ref) = refs[:4], refs[4 : 4 + RING], refs[4 + RING :]
    half, z = place_ref[0], place_ref[1]
    fill_lists(place_ref, index_ref, lists_ref)
    own = lists_ref[pl.ds(z, 1), :]
    shape = (RING, own.shape[1])
    owner = lax.broadcast_in_dim(quotient(own, width), shape, (0, 1))
    target = ((lax.broadcasted_iota(I32, shape, 0) + z) & (RING - 1)) + half * RING
    mask = owner == target
    rank = jnp.where(mask, running(mask) - 1, -1)
    slot = lax.broadcasted_iota(I32, (SLOT, shape[1]), 0)
    for d in range(RING):
        row = lax.broadcast_in_dim(rank[d : d + 1, :], slot.shape, (0, 1))
        sel_ref[d * SLOT : (d + 1) * SLOT, :] = jnp.where(row == slot, 1.0, 0.0).astype(BF16)
    parts = [split(ref[...]) for ref in uppers]
    high = jnp.concatenate([p[0] for p in parts], axis=1)
    low = jnp.concatenate([p[1] for p in parts], axis=1)
    packed = dot(sel_ref[...], high, TRANSPOSED) + dot(sel_ref[...], low, TRANSPOSED)
    for d in range(RING):
        outs[d][...] = packed[d * SLOT : (d + 1) * SLOT, :]


def choose_kernel(width, place_ref, index_ref, sel_ref, most_ref, lists_ref, rank_ref):
    half, z = place_ref[0], place_ref[1]
    me = half * RING + z
    fill_lists(place_ref, index_ref, lists_ref)
    owner = quotient(lists_ref[...], width)
    counts = [jnp.sum(jnp.where(owner == t, 1.0, 0.0), axis=1, keepdims=True) for t in range(2 * RING)]
    most_ref[0] = jnp.max(functools.reduce(jnp.maximum, counts))
    mask = owner == me
    rank_ref[...] = jnp.where(mask, running(mask) - 1, -1)
    per = owner.shape[1] // 2
    slot = lax.broadcasted_iota(I32, (SLOT, per), 0)
    column = lax.broadcasted_iota(I32, (width, per), 0)
    for d in range(RING):
        source = (z - d) & (RING - 1)
        index = lists_ref[pl.ds(source, 1), :] - me * width
        rank = rank_ref[pl.ds(source, 1), :]
        for child in range(2):
            cut = slice(child * per, (child + 1) * per)
            r = lax.broadcast_in_dim(rank[:, cut], slot.shape, (0, 1))
            c = lax.broadcast_in_dim(index[:, cut], column.shape, (0, 1))
            here = jnp.where(r == slot, 1.0, 0.0).astype(BF16)
            there = jnp.where(c == column, 1.0, 0.0).astype(BF16)
            sel_ref[child, d * SLOT : (d + 1) * SLOT, :] = dot(here, there, TRANSPOSED).astype(BF16)


ORDER = [(own, d) for own in (True, False) for d in (0, 1, -1, 2, -2, 3, -3, 4)]
CHUNK = 1024


def tile_of(place_ref, own, distance):
    half, z = place_ref[0], place_ref[1]
    return (half if own else 1 - half) * RING + ((z - distance) & (RING - 1))


LANES = 128


def load_kernel(base_ref, out_ref):
    for h in range(out_ref.shape[1]):
        out_ref[:, h, :] = base_ref[:, h * LANES : (h + 1) * LANES]


def finish_kernel(where, place_ref, index_ref, most_ref, sel_ref, acc_in_ref, *refs):
    slow, refs = refs[:4], refs[4:]
    first_ref, panels, refs = refs[0], refs[1 : 1 + 2 * RING], refs[1 + 2 * RING :]
    out_ref, acc_ref, high_ref, low_ref, inv_ref, factor_ref, upd_ref = refs
    count, order = high_ref.shape
    rows, part = count // (2 * RING), order // (2 * RING)
    halves = acc_ref.shape[1]
    for panel, (own, distance) in zip(panels, ORDER):
        at = pl.multiple_of(tile_of(place_ref, own, distance) * part, part)
        for child in range(2):
            start = 2 * rows + child * part
            inv_ref[child, pl.ds(at, part), :] = panel[start : start + part, :]
    arrived = [first_ref[...]]
    for d in range(1, RING):
        arrived += [panels[k][start : start + size, :] for k, start, size in where[d]]
    upper = split(jnp.concatenate(arrived, axis=0))
    for child in range(2):
        high, low = split(split_dot(split(inv_ref[child]), upper, TRANSPOSED))
        factor_ref[2 * child] = dot(high, sel_ref[child]).astype(BF16)
        factor_ref[2 * child + 1] = dot(low, sel_ref[child]).astype(BF16)

    @pl.when(most_ref[0] > SLOT)
    def _():
        for k in range(4):
            pltpu.sync_copy(slow[k], factor_ref.at[k])

    step = 16
    for child in range(2):
        for k in range(2 * RING):
            high, low = split(panels[k][child * rows : (child + 1) * rows, :])
            high_ref[k * rows : (k + 1) * rows, :] = high
            low_ref[k * rows : (k + 1) * rows, :] = low
        factor = (factor_ref[2 * child], factor_ref[2 * child + 1])
        for start in range(0, count, CHUNK):
            cut = slice(start, start + CHUNK)
            upd = split_dot((high_ref[cut, :], low_ref[cut, :]), factor)
            for h in range(halves):
                upd_ref[cut, h, :] = upd[:, h * LANES : (h + 1) * LANES]
        for k, (own, distance) in enumerate(ORDER):
            base = (child * 2 * RING + tile_of(place_ref, own, distance)) * rows

            def body(i, _, k=k, base=base):
                to = [index_ref[base + i * step + j] for j in range(step)]
                at = k * rows + i * step
                new = [acc_ref[to[j]] - upd_ref[at + j] for j in range(step)]
                for j in range(step):
                    acc_ref[to[j]] = new[j]
                return 0

            lax.fori_loop(0, rows // step, body, 0)
    for h in range(halves):
        out_ref[:, h * LANES : (h + 1) * LANES] = acc_ref[:, h, :]


def vmem():
    return pl.BlockSpec(memory_space=pltpu.VMEM)


def smem():
    return pl.BlockSpec(memory_space=pltpu.SMEM)


def pack(width, place, index_map, uppers):
    depth, per = uppers[0].shape
    return pl.pallas_call(
        functools.partial(pack_kernel, width),
        out_shape=[jax.ShapeDtypeStruct((SLOT, depth), F32)] * RING,
        in_specs=[smem()] + [vmem()] * 5,
        out_specs=[vmem()] * RING,
        scratch_shapes=[pltpu.VMEM((RING, 4 * per), I32), pltpu.VMEM((RING * SLOT, 4 * per), BF16)],
        compiler_params=pltpu.CompilerParams(vmem_limit_bytes=14 * MIB),
        cost_estimate=pl.CostEstimate(flops=2**30, bytes_accessed=2**21, transcendentals=0),
        name="pack",
    )(place, index_map, *uppers)


def choose(width, place, index_map):
    per = index_map.shape[2] // (2 * RING)
    return pl.pallas_call(
        functools.partial(choose_kernel, width),
        out_shape=[jax.ShapeDtypeStruct((2, RING * SLOT, width), BF16), jax.ShapeDtypeStruct((1,), F32)],
        in_specs=[smem(), vmem()],
        out_specs=[vmem(), smem()],
        scratch_shapes=[pltpu.VMEM((RING, 4 * per), I32), pltpu.VMEM((RING, 4 * per), I32)],
        compiler_params=pltpu.CompilerParams(vmem_limit_bytes=14 * MIB),
        cost_estimate=pl.CostEstimate(flops=2**30, bytes_accessed=2**21, transcendentals=0),
        name="choose",
    )(place, index_map)


def load(base):
    return pl.pallas_call(
        load_kernel,
        out_shape=jax.ShapeDtypeStruct((base.shape[0], base.shape[1] // LANES, LANES), F32),
        in_specs=[vmem()],
        out_specs=vmem(),
        compiler_params=pltpu.CompilerParams(vmem_limit_bytes=12 * MIB),
        cost_estimate=pl.CostEstimate(flops=0, bytes_accessed=2**23, transcendentals=0),
        name="load",
    )(base)


def finish(place, index, most, sel, acc, slow, first, panels, where):
    order, count = panels[0].shape[1], index.shape[0] // 2
    width = acc.shape[1] * acc.shape[2]
    return pl.pallas_call(
        functools.partial(finish_kernel, where),
        out_shape=[jax.ShapeDtypeStruct((acc.shape[0], width), F32), jax.ShapeDtypeStruct(acc.shape, F32)],
        in_specs=[smem()] * 3 + [vmem()] * 2 + [pl.BlockSpec(memory_space=pl.ANY)] * 4 + [vmem()] * (1 + 2 * RING),
        out_specs=[vmem()] * 2,
        input_output_aliases={4: 1},
        scratch_shapes=[
            pltpu.VMEM((count, order), BF16),
            pltpu.VMEM((count, order), BF16),
            pltpu.VMEM((2, order, order), F32),
            pltpu.VMEM((4, order, width), BF16),
            pltpu.VMEM((count, *acc.shape[1:]), F32),
        ],
        compiler_params=pltpu.CompilerParams(vmem_limit_bytes=28 * MIB),
        cost_estimate=pl.CostEstimate(flops=2**33, bytes_accessed=2**24, transcendentals=0),
        name="finish",
    )(place, index, most, sel, acc, *slow, first, *panels)[0]


def split_parts(matrix):
    high = matrix.astype(BF16)
    back = lax.optimization_barrier(high).astype(F32)
    return high, (matrix - back).astype(BF16)


def gather(x, axis):
    n = lax.axis_size("tile")
    tile = lax.axis_index("tile")
    size = x.shape[axis]
    whole = jnp.zeros(tuple(n * m if a == axis else m for a, m in enumerate(x.shape)), x.dtype)

    def body(k, state):
        whole, x = state
        whole = lax.dynamic_update_slice_in_dim(whole, x, ((tile - k) % n) * size, axis)
        return whole, lax.ppermute(x, "tile", [(i, (i + 1) % n) for i in range(n)])

    return lax.fori_loop(0, n, body, (whole, x))[0]


def whole_factor(inverse_rows, upper, mapping, col_start, width):
    inverse = gather(inverse_rows, 0)
    full = gather(split_dot(split_parts(inverse), split_parts(upper)), 1)
    high, low = split_parts(full)
    chosen = mapping[:, None] == col_start + jnp.arange(width, dtype=I32)[None, :]
    chosen = chosen.astype(BF16)
    return dot(high, chosen).astype(BF16), dot(low, chosen).astype(BF16)


def shards(pivot_inverse, panel_upper, panel_lower, index_map, parent_base):
    base = parent_base[0]
    width = base.shape[1]
    tile = lax.axis_index("tile")
    group = lax.axis_index("front")
    half, z = tile // RING, tile % RING
    place = jnp.stack([half, z, group]).astype(I32)

    swap = [(i, i ^ 1) for i in range(lax.axis_size("front"))]
    u0, l0, i0 = panel_upper[0, 0], panel_lower[0, 0], pivot_inverse[0, 0]
    i1 = lax.ppermute(pivot_inverse[0, 1], "front", swap)
    l1 = lax.ppermute(panel_lower[0, 1], "front", swap)
    u1 = lax.ppermute(panel_upper[0, 1], "front", swap)
    first = lax.dynamic_index_in_dim(index_map[:, 0], group, 0, keepdims=False)
    second = lax.dynamic_index_in_dim(index_map[:, 1], group ^ 1, 0, keepdims=False)
    index = jnp.concatenate([first, second])

    own, other = {0: jnp.concatenate([l0, l1, i0, i1], axis=0)}, {}
    far0, far1 = across(u0), across(u1)
    own[1], own[-1] = along(own[0], 1), along(own[0], -1)
    sel, most = choose(width, place, index_map)

    def slow_way():
        start = tile * width
        return whole_factor(i0, u0, first, start, width) + whole_factor(i1, u1, second, start, width)

    def fast_way():
        return (jnp.zeros((l0.shape[1], width), BF16),) * 4

    slow = lax.cond(most[0] > SLOT, slow_way, fast_way)
    packed = pack(width, after(place, slow[0]), index_map, [u0, far0, u1, far1])
    acc = load(after(base, packed[1]))

    size, part = own[0].shape[0], SLOT // 2

    def passed_on(x):
        return x[: x.shape[0] - SLOT]

    up = jnp.concatenate([own[1], packed[4][:part], packed[3], packed[2], packed[1]], axis=0)
    down = jnp.concatenate([own[-1], packed[4][part:], packed[5], packed[6], packed[7]], axis=0)
    own[2], own[-2] = along(up, 1), along(down, -1)
    other[0] = across(own[0], far0, packed[1])
    other[1] = across(own[1], far1, packed[1])
    done = other[0], other[1]
    own[3], own[-3] = along(passed_on(own[2]), 1, *done), along(passed_on(own[-2]), -1, *done)
    other[2] = across(own[2][:size], *done)
    done = other[2], own[3], own[-3]
    own[4] = along(passed_on(own[-3]), -1, *done)
    other[3] = along(jnp.concatenate([other[2], own[3][size : size + part + SLOT]], axis=0), 1, *done)
    other[-2] = across(own[-2][:size], *done)
    done = own[4], other[3], other[-2]
    other[4] = along(passed_on(other[3]), 1, *done)
    other[-3] = along(jnp.concatenate([other[-2], own[4][size : size + part]], axis=0), -1, *done)
    other[-1] = across(own[-1], *done)

    panels = [(own if mine else other)[d] for mine, d in ORDER]
    place_of = {x: k for k, x in enumerate(ORDER)}
    near = {1: (True, 2), 2: (True, 3), 3: (False, 3), 7: (True, -2), 6: (True, -3), 5: (True, 4)}
    where = {}
    for d, x in near.items():
        rows = panels[place_of[x]].shape[0]
        where[d] = [(place_of[x], rows - SLOT, SLOT)]
    where[4] = [(place_of[x], size, part) for x in ((False, 4), (False, -3))]
    return finish(place, index, most, sel, acc, slow, packed[0], panels, where)[None]


def solution(mesh):
    return jax.shard_map(
        shards,
        mesh=mesh,
        in_specs=(
            P("front", None, "tile", None),
            P("front", None, None, "tile"),
            P("front", None, "tile", None),
            P(),
            P("front", None, "tile"),
        ),
        out_specs=P("front", None, "tile"),
        check_vma=False,
    )
```

```python
import functools

import jax
import jax.numpy as jnp
from jax import lax
from jax.experimental import pallas as pl
from jax.experimental.pallas import tpu as pltpu
from jax.sharding import PartitionSpec as P

RING = 8
SLOT = 64
MIB = 1024 * 1024
F32, BF16, I32 = jnp.float32, jnp.bfloat16, jnp.int32
TRANSPOSED = (((1,), (1,)), ((), ()))


def shift(distance):
    def to(i):
        return (i // RING) * RING + (i + distance) % RING

    return [(i, to(i)) for i in range(2 * RING)]


ACROSS = [(i, i ^ RING) for i in range(2 * RING)]


def after(value, *done):
    return lax.optimization_barrier((value, *done))[0]


def along(value, distance, *done):
    return lax.ppermute(after(value, *done), "tile", shift(distance))


def across(value, *done):
    return lax.ppermute(after(value, *done), "tile", ACROSS)


def split(x):
    high = x.astype(BF16)
    return high, (x - high.astype(F32)).astype(BF16)


def dot(a, b, dims=(((1,), (0,)), ((), ()))):
    return lax.dot_general(a, b, dims, preferred_element_type=F32)


def split_dot(a, b, dims=(((1,), (0,)), ((), ()))):
    (ah, al), (bh, bl) = a, b
    return dot(ah, bh, dims) + dot(ah, bl, dims) + dot(al, bh, dims)


def quotient(x, divisor):
    assert divisor & (divisor - 1) == 0
    return lax.shift_right_logical(x, jnp.full(x.shape, divisor.bit_length() - 1, x.dtype))


def running(mask):
    n = mask.shape[1]
    upper = lax.broadcasted_iota(I32, (n, n), 0) <= lax.broadcasted_iota(I32, (n, n), 1)
    ones = jnp.where(upper, 1.0, 0.0).astype(BF16)
    return dot(jnp.where(mask, 1.0, 0.0).astype(BF16), ones).astype(I32)


def fill_lists(place_ref, index_ref, lists_ref):
    half, group = place_ref[0], place_ref[2]
    per = lists_ref.shape[1] // 4
    for child, g in ((0, group), (1, jnp.bitwise_xor(group, 1))):
        for k, h in ((0, half), (1, 1 - half)):
            start = pl.multiple_of(h * RING * per, RING * per)
            row = index_ref[pl.ds(g, 1), child, pl.ds(start, RING * per)]
            at = (2 * child + k) * per
            for source in range(RING):
                lists_ref[source : source + 1, at : at + per] = row[:, source * per : (source + 1) * per]


def pack_kernel(width, place_ref, index_ref, *refs):
    uppers, outs, (lists_ref, sel_ref) = refs[:4], refs[4 : 4 + RING], refs[4 + RING :]
    half, z = place_ref[0], place_ref[1]
    fill_lists(place_ref, index_ref, lists_ref)
    own = lists_ref[pl.ds(z, 1), :]
    shape = (RING, own.shape[1])
    owner = lax.broadcast_in_dim(quotient(own, width), shape, (0, 1))
    target = ((lax.broadcasted_iota(I32, shape, 0) + z) & (RING - 1)) + half * RING
    mask = owner == target
    rank = jnp.where(mask, running(mask) - 1, -1)
    slot = lax.broadcasted_iota(I32, (SLOT, shape[1]), 0)
    for d in range(RING):
        row = lax.broadcast_in_dim(rank[d : d + 1, :], slot.shape, (0, 1))
        sel_ref[d * SLOT : (d + 1) * SLOT, :] = jnp.where(row == slot, 1.0, 0.0).astype(BF16)
    parts = [split(ref[...]) for ref in uppers]
    high = jnp.concatenate([p[0] for p in parts], axis=1)
    low = jnp.concatenate([p[1] for p in parts], axis=1)
    packed = dot(sel_ref[...], high, TRANSPOSED) + dot(sel_ref[...], low, TRANSPOSED)
    for d in range(RING):
        outs[d][...] = packed[d * SLOT : (d + 1) * SLOT, :]


def choose_kernel(width, place_ref, index_ref, sel_ref, most_ref, lists_ref, rank_ref):
    half, z = place_ref[0], place_ref[1]
    me = half * RING + z
    fill_lists(place_ref, index_ref, lists_ref)
    owner = quotient(lists_ref[...], width)
    counts = [jnp.sum(jnp.where(owner == t, 1.0, 0.0), axis=1, keepdims=True) for t in range(2 * RING)]
    most_ref[0] = jnp.max(functools.reduce(jnp.maximum, counts))
    mask = owner == me
    rank_ref[...] = jnp.where(mask, running(mask) - 1, -1)
    per = owner.shape[1] // 2
    slot = lax.broadcasted_iota(I32, (SLOT, per), 0)
    column = lax.broadcasted_iota(I32, (width, per), 0)
    for d in range(RING):
        source = (z - d) & (RING - 1)
        index = lists_ref[pl.ds(source, 1), :] - me * width
        rank = rank_ref[pl.ds(source, 1), :]
        for child in range(2):
            cut = slice(child * per, (child + 1) * per)
            r = lax.broadcast_in_dim(rank[:, cut], slot.shape, (0, 1))
            c = lax.broadcast_in_dim(index[:, cut], column.shape, (0, 1))
            here = jnp.where(r == slot, 1.0, 0.0).astype(BF16)
            there = jnp.where(c == column, 1.0, 0.0).astype(BF16)
            sel_ref[child, d * SLOT : (d + 1) * SLOT, :] = dot(here, there, TRANSPOSED).astype(BF16)


ORDER = [(own, d) for own in (True, False) for d in (0, 1, -1, 2, -2, 3, -3, 4)]
CHUNK = 1024


def tile_of(place_ref, own, distance):
    half, z = place_ref[0], place_ref[1]
    return (half if own else 1 - half) * RING + ((z - distance) & (RING - 1))


LANES = 128


def load_kernel(base_ref, out_ref):
    for h in range(out_ref.shape[1]):
        out_ref[:, h, :] = base_ref[:, h * LANES : (h + 1) * LANES]


def finish_kernel(where, place_ref, index_ref, most_ref, sel_ref, acc_in_ref, *refs):
    slow, refs = refs[:4], refs[4:]
    first_ref, panels, refs = refs[0], refs[1 : 1 + 2 * RING], refs[1 + 2 * RING :]
    out_ref, acc_ref, high_ref, low_ref, inv_ref, factor_ref, upd_ref = refs
    count, order = high_ref.shape
    rows, part = count // (2 * RING), order // (2 * RING)
    halves = acc_ref.shape[1]
    for panel, (own, distance) in zip(panels, ORDER):
        at = pl.multiple_of(tile_of(place_ref, own, distance) * part, part)
        for child in range(2):
            start = 2 * rows + child * part
            inv_ref[child, pl.ds(at, part), :] = panel[start : start + part, :]
    arrived = [first_ref[...]]
    for d in range(1, RING):
        arrived += [panels[k][start : start + size, :] for k, start, size in where[d]]
    upper = split(jnp.concatenate(arrived, axis=0))
    for child in range(2):
        high, low = split(split_dot(split(inv_ref[child]), upper, TRANSPOSED))
        factor_ref[2 * child] = dot(high, sel_ref[child]).astype(BF16)
        factor_ref[2 * child + 1] = dot(low, sel_ref[child]).astype(BF16)

    @pl.when(most_ref[0] > SLOT)
    def _():
        for k in range(4):
            pltpu.sync_copy(slow[k], factor_ref.at[k])

    step = 16
    for child in range(2):
        for k in range(2 * RING):
            high, low = split(panels[k][child * rows : (child + 1) * rows, :])
            high_ref[k * rows : (k + 1) * rows, :] = high
            low_ref[k * rows : (k + 1) * rows, :] = low
        factor = (factor_ref[2 * child], factor_ref[2 * child + 1])
        for start in range(0, count, CHUNK):
            cut = slice(start, start + CHUNK)
            upd = split_dot((high_ref[cut, :], low_ref[cut, :]), factor)
            for h in range(halves):
                upd_ref[cut, h, :] = upd[:, h * LANES : (h + 1) * LANES]
        for k, (own, distance) in enumerate(ORDER):
            base = (child * 2 * RING + tile_of(place_ref, own, distance)) * rows

            def body(i, _, k=k, base=base):
                to = [index_ref[base + i * step + j] for j in range(step)]
                at = k * rows + i * step
                new = [acc_ref[to[j]] - upd_ref[at + j] for j in range(step)]
                for j in range(step):
                    acc_ref[to[j]] = new[j]
                return 0

            lax.fori_loop(0, rows // step, body, 0)
    for h in range(halves):
        out_ref[:, h * LANES : (h + 1) * LANES] = acc_ref[:, h, :]


def vmem():
    return pl.BlockSpec(memory_space=pltpu.VMEM)


def smem():
    return pl.BlockSpec(memory_space=pltpu.SMEM)


def pack(width, place, index_map, uppers):
    depth, per = uppers[0].shape
    return pl.pallas_call(
        functools.partial(pack_kernel, width),
        out_shape=[jax.ShapeDtypeStruct((SLOT, depth), F32)] * RING,
        in_specs=[smem()] + [vmem()] * 5,
        out_specs=[vmem()] * RING,
        scratch_shapes=[pltpu.VMEM((RING, 4 * per), I32), pltpu.VMEM((RING * SLOT, 4 * per), BF16)],
        compiler_params=pltpu.CompilerParams(vmem_limit_bytes=14 * MIB),
        cost_estimate=pl.CostEstimate(flops=2**30, bytes_accessed=2**21, transcendentals=0),
        name="pack",
    )(place, index_map, *uppers)


def choose(width, place, index_map):
    per = index_map.shape[2] // (2 * RING)
    return pl.pallas_call(
        functools.partial(choose_kernel, width),
        out_shape=[jax.ShapeDtypeStruct((2, RING * SLOT, width), BF16), jax.ShapeDtypeStruct((1,), F32)],
        in_specs=[smem(), vmem()],
        out_specs=[vmem(), smem()],
        scratch_shapes=[pltpu.VMEM((RING, 4 * per), I32), pltpu.VMEM((RING, 4 * per), I32)],
        compiler_params=pltpu.CompilerParams(vmem_limit_bytes=14 * MIB),
        cost_estimate=pl.CostEstimate(flops=2**30, bytes_accessed=2**21, transcendentals=0),
        name="choose",
    )(place, index_map)


def load(base):
    return pl.pallas_call(
        load_kernel,
        out_shape=jax.ShapeDtypeStruct((base.shape[0], base.shape[1] // LANES, LANES), F32),
        in_specs=[vmem()],
        out_specs=vmem(),
        compiler_params=pltpu.CompilerParams(vmem_limit_bytes=12 * MIB),
        cost_estimate=pl.CostEstimate(flops=0, bytes_accessed=2**23, transcendentals=0),
        name="load",
    )(base)


def finish(place, index, most, sel, acc, slow, first, panels, where):
    order, count = panels[0].shape[1], index.shape[0] // 2
    width = acc.shape[1] * acc.shape[2]
    return pl.pallas_call(
        functools.partial(finish_kernel, where),
        out_shape=[jax.ShapeDtypeStruct((acc.shape[0], width), F32), jax.ShapeDtypeStruct(acc.shape, F32)],
        in_specs=[smem()] * 3 + [vmem()] * 2 + [pl.BlockSpec(memory_space=pl.ANY)] * 4 + [vmem()] * (1 + 2 * RING),
        out_specs=[vmem()] * 2,
        input_output_aliases={4: 1},
        scratch_shapes=[
            pltpu.VMEM((count, order), BF16),
            pltpu.VMEM((count, order), BF16),
            pltpu.VMEM((2, order, order), F32),
            pltpu.VMEM((4, order, width), BF16),
            pltpu.VMEM((count, *acc.shape[1:]), F32),
        ],
        compiler_params=pltpu.CompilerParams(vmem_limit_bytes=28 * MIB),
        cost_estimate=pl.CostEstimate(flops=2**33, bytes_accessed=2**24, transcendentals=0),
        name="finish",
    )(place, index, most, sel, acc, *slow, first, *panels)[0]


def split_parts(matrix):
    high = matrix.astype(BF16)
    back = lax.optimization_barrier(high).astype(F32)
    return high, (matrix - back).astype(BF16)


def gather(x, axis):
    n = lax.axis_size("tile")
    tile = lax.axis_index("tile")
    size = x.shape[axis]
    whole = jnp.zeros(tuple(n * m if a == axis else m for a, m in enumerate(x.shape)), x.dtype)

    def body(k, state):
        whole, x = state
        whole = lax.dynamic_update_slice_in_dim(whole, x, ((tile - k) % n) * size, axis)
        return whole, lax.ppermute(x, "tile", [(i, (i + 1) % n) for i in range(n)])

    return lax.fori_loop(0, n, body, (whole, x))[0]


def whole_factor(inverse_rows, upper, mapping, col_start, width):
    inverse = gather(inverse_rows, 0)
    full = gather(split_dot(split_parts(inverse), split_parts(upper)), 1)
    high, low = split_parts(full)
    chosen = mapping[:, None] == col_start + jnp.arange(width, dtype=I32)[None, :]
    chosen = chosen.astype(BF16)
    return dot(high, chosen).astype(BF16), dot(low, chosen).astype(BF16)


def shards(pivot_inverse, panel_upper, panel_lower, index_map, parent_base):
    base = parent_base[0]
    width = base.shape[1]
    tile = lax.axis_index("tile")
    group = lax.axis_index("front")
    half, z = tile // RING, tile % RING
    place = jnp.stack([half, z, group]).astype(I32)

    swap = [(i, i ^ 1) for i in range(lax.axis_size("front"))]
    u0, l0, i0 = panel_upper[0, 0], panel_lower[0, 0], pivot_inverse[0, 0]
    i1 = lax.ppermute(pivot_inverse[0, 1], "front", swap)
    l1 = lax.ppermute(panel_lower[0, 1], "front", swap)
    u1 = lax.ppermute(panel_upper[0, 1], "front", swap)
    first = lax.dynamic_index_in_dim(index_map[:, 0], group, 0, keepdims=False)
    second = lax.dynamic_index_in_dim(index_map[:, 1], group ^ 1, 0, keepdims=False)
    index = jnp.concatenate([first, second])

    own, other = {0: jnp.concatenate([l0, l1, i0, i1], axis=0)}, {}
    far0, far1 = across(u0), across(u1)
    own[1], own[-1] = along(own[0], 1), along(own[0], -1)
    sel, most = choose(width, place, index_map)

    def slow_way():
        start = tile * width
        return whole_factor(i0, u0, first, start, width) + whole_factor(i1, u1, second, start, width)

    def fast_way():
        return (jnp.zeros((l0.shape[1], width), BF16),) * 4

    slow = lax.cond(most[0] > SLOT, slow_way, fast_way)
    packed = pack(width, after(place, slow[0]), index_map, [u0, far0, u1, far1])
    acc = load(after(base, packed[1]))

    size, part = own[0].shape[0], SLOT // 2

    def passed_on(x):
        return x[: x.shape[0] - SLOT]

    up = jnp.concatenate([own[1], packed[4][:part], packed[3], packed[2], packed[1]], axis=0)
    down = jnp.concatenate([own[-1], packed[4][part:], packed[5], packed[6], packed[7]], axis=0)
    middle = size // 2
    early = across(own[0][:middle], far0)
    own[2], own[-2] = along(up, 1, early), along(down, -1, early)
    other[0] = jnp.concatenate([early, across(own[0][middle:], far1, packed[1])], axis=0)
    other[1] = across(own[1], far1, packed[1])
    done = other[0], other[1]
    own[3], own[-3] = along(passed_on(own[2]), 1, *done), along(passed_on(own[-2]), -1, *done)
    other[2] = across(own[2][:size], *done)
    done = other[2], own[3], own[-3]
    own[4] = along(passed_on(own[-3]), -1, *done)
    other[3] = along(jnp.concatenate([other[2], own[3][size : size + part + SLOT]], axis=0), 1, *done)
    other[-2] = across(own[-2][:size], *done)
    done = own[4], other[3], other[-2]
    other[4] = along(passed_on(other[3]), 1, *done)
    other[-3] = along(jnp.concatenate([other[-2], own[4][size : size + part]], axis=0), -1, *done)
    other[-1] = across(own[-1], *done)

    panels = [(own if mine else other)[d] for mine, d in ORDER]
    place_of = {x: k for k, x in enumerate(ORDER)}
    near = {1: (True, 2), 2: (True, 3), 3: (False, 3), 7: (True, -2), 6: (True, -3), 5: (True, 4)}
    where = {}
    for d, x in near.items():
        rows = panels[place_of[x]].shape[0]
        where[d] = [(place_of[x], rows - SLOT, SLOT)]
    where[4] = [(place_of[x], size, part) for x in ((False, 4), (False, -3))]
    return finish(place, index, most, sel, acc, slow, packed[0], panels, where)[None]


def solution(mesh):
    return jax.shard_map(
        shards,
        mesh=mesh,
        in_specs=(
            P("front", None, "tile", None),
            P("front", None, None, "tile"),
            P("front", None, "tile", None),
            P(),
            P("front", None, "tile"),
        ),
        out_specs=P("front", None, "tile"),
        check_vma=False,
    )
```
